32 devices in a mesh: groups: 2 (over y), dp: 4 (over z), section: 2 (over x), tensor: 2 (over core).
Axes of the slice: x: 2, y: 2, z: 4, core: 2. Of those that a mesh axis runs over, the one named last changes fastest.
Arguments:
- x_in: bfloat16 [4, 128, 8192], P('groups', None, ('dp', 'tensor')), parts along dimension 0, may hold values from -100 to 100
- subtree_end: int32 [4, 128], P('groups'), parts along dimension 0, may hold values from 0 to 127, as said below
- norm_gain: bfloat16 [2, 8192], P('section', ('dp', 'tensor')), may hold values from 0.5 to 1.5
- w_query: bfloat16 [2, 8192, 1024], P('section', None, ('dp', 'tensor')), may hold values from -1 to 1
- w_kv: bfloat16 [2, 8192, 256], P('section', None, ('dp', 'tensor')), may hold values from -20 to 20
- w_out: bfloat16 [2, 1024, 8192], P('section', None, ('dp', 'tensor')), may hold values from -0.1875 to 0.1875
- a_query: bfloat16 [2, 8192, 64], P('section'), may hold values from -0.0625 to 0.0625
- b_query: bfloat16 [2, 64, 1024], P('section', None, ('dp', 'tensor')), may hold values from -0.75 to 0.75
- a_out: bfloat16 [2, 1024, 64], P('section'), may hold values from -0.1875 to 0.1875
- b_out: bfloat16 [2, 64, 8192], P('section', None, ('dp', 'tensor')), may hold values from -0.75 to 0.75
- grad_a_query: float32 [2, 4, 8192, 64], P('section', 'dp'), may hold values from -0.03125 to 0.03125
- grad_b_query: float32 [2, 4, 64, 1024], P('section', 'dp'), may hold values from -0.5 to 0.5
- grad_a_out: float32 [2, 4, 1024, 64], P('section', 'dp'), may hold values from -0.09375 to 0.09375
- grad_b_out: float32 [2, 4, 64, 8192], P('section', 'dp'), may hold values from -0.5 to 0.5
Outputs:
- hidden_states: bfloat16 [2, 4, 128, 8192], P('section', 'groups', None, ('dp', 'tensor')), parts along dimension 1
The draws below stay inside these ranges and needn't reach their ends.
There are 2 independent parts, one for each index of `groups`. The reference program is written for one: setup_inputs(seed, part) draws one part's arguments, and reference() takes and returns one part's arrays. A program takes and returns all parts, laid end to end along the dimension named above; an argument that names none is the same for every part. Nothing has to cross between parts.
Inputs may be any that keep to these rules, and one draw needn't show every extreme that they name: Tokens stand in depth-first order of one tree rooted at position 0; the descendants of token j are exactly positions j + 1 to subtree_end[m, j].
All inputs are finite; a program needn't handle non-finite values.
Results may differ from the reference program's by a relative error of at most 0.0077.
Values may be sent and summed in bfloat16 or wider, within the bound.
A program may use at most 64 MiB of HBM per device.

```python
import math
import jax
import jax.numpy as jnp
from jax import lax

D = 8192
HD = 128
GROUP = 8
R = 64
TOK = 128
M = 2
SECTIONS = 2
HQ = 8
HK = 1
QW = 1024
KW = 256
N_DP = 4


def shared_query(key):
    return jnp.clip(jax.random.normal(key, (SECTIONS, D, QW), jnp.float32), -6.0, 6.0)


def draw_w_query(key, part):
    base = shared_query(key)
    return (base * D ** (-0.5)).astype(jnp.bfloat16)


def draw_w_kv(key, part):
    key = jax.random.fold_in(key, 2)
    fresh = jnp.clip(jax.random.normal(key, (SECTIONS, D, HK, 2, HD), jnp.float32), -6.0, 6.0)
    return (fresh.reshape(SECTIONS, D, KW) * D ** (-0.5)).astype(jnp.bfloat16)


def draw_x_in(key, part):
    key = jax.random.fold_in(key, 3)
    first = jax.random.fold_in(key, 0)
    cols = jnp.exp(math.log(3.0) * jnp.arange(D, dtype=jnp.float32) / (D - 1))
    base = jnp.clip(jax.random.normal(first, (M, TOK, D), jnp.float32), -6.0, 6.0)
    return (base * cols).astype(jnp.bfloat16)


def one_tree(key):
    upward, picking = jax.random.split(key)
    climbs = jax.random.randint(upward, (TOK,), 0, 4)
    picks = jax.random.randint(picking, (TOK,), 0, 1 << 20)

    def step(prior, inputs):
        climb, pick = inputs
        depth = jnp.where(climb < 3, prior + 1, 1 + pick % (prior + 1))
        return (depth, depth)
    _, rest = lax.scan(step, jnp.int32(0), (climbs[1:], picks[1:]))
    depth = jnp.concatenate([jnp.zeros((1,), jnp.int32), rest])
    places = jnp.arange(TOK, dtype=jnp.int32)
    later = (places[None, :] > places[:, None]) & (depth[None, :] <= depth[:, None])
    stop = jnp.min(jnp.where(later, places[None, :], TOK), axis=1)
    return (stop - 1).astype(jnp.int32)


def draw_subtree_end(key, part):
    key = jax.random.fold_in(key, 4)
    return jax.vmap(one_tree)(jax.random.split(key, M))


def with_spikes(array, own_key, source, target, blocks, factor):
    def block_of(position):
        return (jnp.arange(array.shape[position]) // (array.shape[position] // blocks)).reshape((-1,) + (1,) * (array.ndim - 1 - position))

    one_side = jax.random.permutation(own_key, blocks)[block_of(target)]
    other_side = (block_of(target) + blocks // 2) % blocks
    return jnp.where((block_of(source) == one_side) | (block_of(source) == other_side), factor * array, array)


def steps_of(key, extent, cuts, low, top_value):
    loudness = 1.0
    for position, blocks in cuts:
        draws = jax.random.uniform(jax.random.fold_in(jax.random.fold_in(key, 6), position), (blocks,), jnp.float32, low / len(cuts), top_value / len(cuts))
        loudness = loudness * jnp.repeat(jnp.exp(draws), extent[position] // blocks).reshape((-1,) + (1,) * (len(extent) - 1 - position))
    return loudness


def noise(own_key, shape, scale, limit, cuts=(), kind=jnp.bfloat16):
    drawn = scale * jax.random.normal(own_key, shape, jnp.float32)
    if cuts:
        drawn = drawn * steps_of(own_key, shape, cuts, -0.22, 0.18)
    return jnp.clip(drawn, -limit, limit).astype(kind)


def noise_with(key, dims, spread, limit, shards, heavy, kind=jnp.bfloat16):
    result = spread * jax.random.normal(key, dims, jnp.float32)
    if shards:
        result = result * steps_of(key, dims, shards, -0.22, 0.18)
    return jnp.clip(with_spikes(result, jax.random.fold_in(key, 3), *heavy), -limit, limit).astype(kind)


def setup_inputs(seed: int = 0, part: int = 0) -> dict:
    key_of = jax.random.split(jax.random.key(seed), 15)
    own_keys = jax.random.split(jax.random.fold_in(key_of[14], part), 15)
    return {
        "x_in": draw_x_in(jax.random.fold_in(jax.random.fold_in(key_of[14], part), 71), part),
        "subtree_end": draw_subtree_end(jax.random.fold_in(jax.random.fold_in(key_of[14], part), 71), part),
        "norm_gain": jnp.clip(1.0 + 0.1 * jax.random.normal(key_of[2], (SECTIONS, D), jnp.float32), 0.5, 1.5).astype(jnp.bfloat16),
        "w_query": draw_w_query(jax.random.fold_in(key_of[14], 71), part),
        "w_kv": draw_w_kv(jax.random.fold_in(key_of[14], 71), part),
        "w_out": noise(key_of[5], (SECTIONS, QW, D), QW ** -0.5, 0.1875, ((0, 2), (2, 8))),
        "a_query": noise(key_of[6], (SECTIONS, D, R), D ** -0.5, 0.0625, ((0, 2),)),
        "b_query": noise(key_of[7], (SECTIONS, R, QW), R ** -0.5, 0.75, ((0, 2), (2, 8))),
        "a_out": noise(key_of[8], (SECTIONS, QW, R), QW ** -0.5, 0.1875, ((0, 2),)),
        "b_out": noise(key_of[9], (SECTIONS, R, D), R ** -0.5, 0.75, ((0, 2), (2, 8))),
        "grad_a_query": noise(key_of[10], (SECTIONS, N_DP, D, R), ((D * N_DP) ** -0.5), 0.03125, ((0, 2), (1, 4)), jnp.float32),
        "grad_b_query": noise_with(key_of[11], (SECTIONS, N_DP, R, QW), ((R * N_DP) ** -0.5), 0.5, ((0, 2), (1, 4)), (1, 3, 4, 2.0), jnp.float32),
        "grad_a_out": noise(key_of[12], (SECTIONS, N_DP, QW, R), ((QW * N_DP) ** -0.5), 0.09375, ((0, 2), (1, 4)), jnp.float32),
        "grad_b_out": noise_with(key_of[13], (SECTIONS, N_DP, R, D), ((R * N_DP) ** -0.5), 0.5, ((0, 2), (1, 4)), (1, 3, 4, 2.0), jnp.float32),
    }


RATE = 0.5
EPS = 1e-05

def one_layer(hidden, ends, gain, merged_q, w_kv, merged_o):
    wide = hidden.astype(jnp.float32)
    scaled = (wide * gain.astype(jnp.float32)).astype(jnp.bfloat16)
    inverse = lax.rsqrt(lax.optimization_barrier(jnp.sum(wide * wide, axis=1)) / D + EPS)[:, None]
    query = (jnp.dot(scaled, merged_q, preferred_element_type=jnp.float32) * inverse).astype(jnp.bfloat16)
    kv_rows = (jnp.dot(scaled, w_kv, preferred_element_type=jnp.float32) * inverse).astype(jnp.bfloat16)
    query = query.reshape(TOK, HQ, HD).astype(jnp.float32)
    kv_rows = kv_rows.reshape(TOK, HK, 2, HD).astype(jnp.float32)
    keys = jnp.repeat(kv_rows[:, :, 0, :], GROUP, axis=1)
    values = jnp.repeat(kv_rows[:, :, 1, :], GROUP, axis=1)
    scores = jnp.einsum('qhd,khd->hqk', query, keys) * HD ** (-0.5)
    places = jnp.arange(TOK)
    visible = (places[None, :] <= places[:, None]) & (ends[None, :] >= places[:, None])
    scores = jnp.where(visible[None], scores, -1e+30)
    top = lax.optimization_barrier(jnp.max(scores, axis=-1, keepdims=True))
    weights = jnp.exp(scores - top)
    weights = (weights / lax.optimization_barrier(jnp.sum(weights, axis=-1, keepdims=True))).astype(jnp.bfloat16)
    mixed = jnp.einsum('hqk,khd->qhd', weights.astype(jnp.float32), values)
    mixed = mixed.astype(jnp.bfloat16).reshape(TOK, QW)
    total = jnp.dot(mixed, merged_o, preferred_element_type=jnp.float32)
    return (wide + total).astype(jnp.bfloat16)

def updated(factor, grads):
    return (factor.astype(jnp.float32) - RATE * lax.optimization_barrier(jnp.sum(grads, axis=1))).astype(jnp.bfloat16)

def reference(x_in, subtree_end, norm_gain, w_query, w_kv, w_out, a_query, b_query, a_out, b_out, grad_a_query, grad_b_query, grad_a_out, grad_b_out):
    new_aq = updated(a_query, grad_a_query)
    new_bq = updated(b_query, grad_b_query)
    new_ao = updated(a_out, grad_a_out)
    new_bo = updated(b_out, grad_b_out)
    hidden = x_in
    results = []
    for layer in range(SECTIONS):
        merged_q = (w_query[layer].astype(jnp.float32) + jnp.dot(new_aq[layer], new_bq[layer], preferred_element_type=jnp.float32)).astype(jnp.bfloat16)
        merged_o = (w_out[layer].astype(jnp.float32) + jnp.dot(new_ao[layer], new_bo[layer], preferred_element_type=jnp.float32)).astype(jnp.bfloat16)
        apply_one = lambda rows, ends: one_layer(rows, ends, norm_gain[layer], merged_q, w_kv[layer], merged_o)
        hidden = jax.vmap(apply_one)(hidden, subtree_end)
        results.append(hidden)
    return jnp.stack(results)
```

```python
import functools

import jax
import jax.numpy as jnp
from jax import lax
from jax.experimental import pallas as pl
from jax.experimental.pallas import tpu as pltpu
from jax.sharding import PartitionSpec as P

HD = 128
GROUP = 8
RATE = 0.5
EPS = 1e-05
MESH = pl.DeviceIdType.MESH
F32 = jnp.float32
BF16 = jnp.bfloat16


def chain(
    sizes,
    x_ref,
    ends_ref,
    gain_ref,
    g_ref,
    base_ref,
    wq_hbm,
    wx_hbm,
    wo_hbm,
    out_ref,
    wcat,
    merged,
    blocks,
    squares,
    hidden,
    kvx,
    mix,
    grecv,
    aot,
    bo,
    bpad,
    acc,
    scaled_q,
    w_sem,
    blk_send,
    blk_fwd,
    blk_recv,
    sq_send,
    sq_recv,
    kv_send,
    kv_recv,
    mix_send,
    mix_recv,
    g_send,
    g_recv,
    ao_send,
    ao_recv,
    hid_send,
    hid_recv,
):
    n_dp, n_section, kv_cols = sizes
    n = 2 * n_dp
    micro, tok, feat = x_ref.shape
    rank = base_ref.shape[0]
    width = n * feat
    d, t, s = lax.axis_index("dp"), lax.axis_index("tensor"), lax.axis_index("section")
    me = 2 * d + t

    def peer(k):
        return lax.rem(me + k, n)

    def place(i):
        return {"dp": i // 2, "tensor": lax.rem(i, 2)}

    def along(k):
        return lax.rem(d + k, n_dp)

    def loop(low, high, body):
        def step(k, carry):
            body(k)
            return carry

        lax.fori_loop(low, high, step, jnp.int32(0))

    def weights(k):
        if k == 0:
            return pltpu.make_async_copy(wq_hbm, wcat.at[:, pl.ds(0, HD)], w_sem.at[0])
        if k == 1:
            return pltpu.make_async_copy(wx_hbm, wcat.at[:, pl.ds(HD, HD)], w_sem.at[1])
        return pltpu.make_async_copy(wo_hbm, merged, w_sem.at[2])

    def block_copy(m, i, send, to):
        return pltpu.make_async_remote_copy(
            src_ref=blocks.at[m, i],
            dst_ref=blocks.at[m, i],
            send_sem=send,
            recv_sem=blk_recv.at[m, i],
            device_id=to,
            device_id_type=MESH,
        )

    def to_shard(m, k):
        return block_copy(m, me, blk_send.at[m, k], {"dp": along(k), "tensor": t})

    def to_sibling(m):
        return block_copy(m, me, blk_send.at[m, 0], {"tensor": 1 - t})

    def forward(m, k):
        return block_copy(m, 2 * along(k) + t, blk_fwd.at[m, k], {"tensor": 1 - t})

    def spread(buffer, send, recv, k, i):
        return pltpu.make_async_remote_copy(
            src_ref=buffer.at[i],
            dst_ref=buffer.at[i],
            send_sem=send.at[k],
            recv_sem=recv.at[i],
            device_id=place(peer(k)),
            device_id_type=MESH,
        )

    small = (
        lambda m: (squares.at[m], sq_send.at[m], sq_recv.at[m]),
        lambda m: (kvx.at[m], kv_send.at[m], kv_recv.at[m]),
        lambda m: (mix.at[m], mix_send.at[m], mix_recv.at[m]),
        lambda m: (aot, ao_send, ao_recv),
    )

    def start_all(kind, m):
        loop(1, n, lambda k: spread(*small[kind](m), k, me).start())

    def arrive_all(kind, m):
        loop(1, n, lambda k: spread(*small[kind](m), k, peer(k)).wait_recv())

    def sent_all(kind, m):
        loop(1, n, lambda k: spread(*small[kind](m), k, me).wait_send())

    def grads(k):
        return pltpu.make_async_remote_copy(
            src_ref=g_ref.at[2 * along(k) + t],
            dst_ref=grecv.at[d],
            send_sem=g_send.at[k],
            recv_sem=g_recv.at[d],
            device_id={"dp": along(k), "tensor": t},
            device_id_type=MESH,
        )

    def grads_in(k):
        return pltpu.make_async_remote_copy(
            src_ref=g_ref.at[me],
            dst_ref=grecv.at[along(k)],
            send_sem=g_send.at[k],
            recv_sem=g_recv.at[along(k)],
            device_id={"dp": along(k), "tensor": t},
            device_id_type=MESH,
        )

    def onward(m, to):
        return pltpu.make_async_remote_copy(
            src_ref=out_ref.at[m],
            dst_ref=hidden.at[m],
            send_sem=hid_send.at[m],
            recv_sem=hid_recv.at[m],
            device_id={"section": to},
            device_id_type=MESH,
        )

    def enter(m):
        wide = hidden[m].astype(F32)
        blocks[m, me] = (wide * gain_ref[...]).astype(BF16)
        to_sibling(m).start()
        loop(1, n_dp, lambda k: to_shard(m, k).start())
        column = jnp.sum(wide * wide, axis=1, keepdims=True)
        squares[m, me] = jnp.transpose(jnp.broadcast_to(column, (tok, HD)))[:8]
        start_all(0, m)

    def enter_first(m):
        hidden[m] = x_ref[m]
        enter(m)

    def enter_later(m):
        onward(m, jnp.maximum(s - 1, 0)).wait_recv()
        enter(m)

    def project_block(m, i):
        rows = pl.ds(pl.multiple_of(i * feat, feat), feat)
        acc[...] += jnp.dot(blocks[m, i], wcat[rows, :], preferred_element_type=F32)

    def project(m):
        if m == 0:
            weights(0).wait()
            weights(1).wait()
        acc[...] = jnp.zeros_like(acc)
        project_block(m, me)

        def near(k):
            i = 2 * along(k) + t
            block_copy(m, i, blk_send.at[m, k], {"tensor": 1 - t}).wait_recv()
            forward(m, k).start()
            project_block(m, i)

        def far(k):
            i = 2 * along(k) + 1 - t
            block_copy(m, i, blk_send.at[m, k], {"tensor": 1 - t}).wait_recv()
            project_block(m, i)

        loop(1, n_dp, near)
        loop(0, n_dp, far)
        arrive_all(0, m)
        total = jnp.sum(squares[m], axis=0)[:1]
        column = jnp.transpose(jnp.broadcast_to(total, (tok, HD)))
        inverse = lax.rsqrt(column / width + EPS)
        scaled_q[...] = acc[:, :HD] * inverse
        kvx[m, me] = (acc[:, HD:] * inverse).astype(BF16)
        start_all(1, m)

    def update():
        total = g_ref[me].astype(F32)
        loop(1, n_dp, lambda k: grads_in(k).wait_recv())
        for k in range(1, n_dp):
            total = total + grecv[along(k)].astype(F32)
        fresh = (base_ref[...].astype(F32) - RATE * total).astype(BF16)
        bo[...] = fresh[:, :feat]
        bpad[...] = jnp.zeros_like(bpad)
        bpad[pl.ds(kv_cols, rank), :] = fresh[:, feat : feat + HD]
        aot[me] = fresh[:, feat + HD :]
        start_all(3, 0)

    def merge():
        weights(2).wait()
        arrive_all(3, 0)

        def rows_of(j):
            rows = pl.ds(pl.multiple_of(j * HD, HD), HD)
            product = lax.dot_general(
                aot[j], bo[...], (((0,), (0,)), ((), ())), preferred_element_type=F32
            )
            merged[rows, :] = (merged[rows, :].astype(F32) + product).astype(BF16)

        loop(0, n, rows_of)

    def attend(m):
        arrive_all(1, m)
        query = scaled_q[...]
        for k in range(n_dp):
            query = query + jnp.dot(kvx[m, 2 * k + t], bpad[...], preferred_element_type=F32)
        query = query.astype(BF16)
        per = HD // kv_cols
        first = me // GROUP * 2 * per
        spot = lax.broadcasted_iota(jnp.int32, (HD, HD), 0)
        lane = lax.broadcasted_iota(jnp.int32, (HD, HD), 1)
        keys = jnp.zeros((tok, HD), F32)
        values = jnp.zeros((tok, HD), F32)
        for i in range(per):
            pick = jnp.where((spot < kv_cols) & (lane == spot + i * kv_cols), 1.0, 0.0).astype(BF16)
            keys = keys + jnp.dot(kvx[m, first + i], pick, preferred_element_type=F32)
            values = values + jnp.dot(kvx[m, first + per + i], pick, preferred_element_type=F32)
        scores = lax.dot_general(
            query, keys.astype(BF16), (((1,), (1,)), ((), ())), preferred_element_type=F32
        ) * HD ** (-0.5)
        here = lax.broadcasted_iota(jnp.int32, (tok, tok), 0)
        there = lax.broadcasted_iota(jnp.int32, (tok, tok), 1)
        visible = (there <= here) & (ends_ref[m] >= here)
        scores = jnp.where(visible, scores, -1e30)
        raised = jnp.exp(scores - jnp.max(scores, axis=-1, keepdims=True))
        portion = (raised / jnp.sum(raised, axis=-1, keepdims=True)).astype(BF16)
        mixed = jnp.dot(portion, values.astype(BF16), preferred_element_type=F32)
        mix[m, me] = mixed.astype(BF16)
        start_all(2, m)

    def leave(m):
        arrive_all(2, m)
        heads = jnp.concatenate([mix[m, j] for j in range(n)], axis=1)
        total = jnp.dot(heads, merged[...], preferred_element_type=F32)
        out_ref[m] = (hidden[m].astype(F32) + total).astype(BF16)

        @pl.when(s < n_section - 1)
        def _():
            onward(m, jnp.minimum(s + 1, n_section - 1)).start()

    for k in range(3):
        weights(k).start()
    barrier = pltpu.get_barrier_semaphore()

    def greet(k):
        pl.semaphore_signal(barrier, inc=1, device_id=place(peer(k)), device_id_type=MESH)

    loop(1, n, greet)

    @pl.when(s > 0)
    def _():
        pl.semaphore_signal(barrier, inc=1, device_id={"section": s - 1}, device_id_type=MESH)

    @pl.when(s < n_section - 1)
    def _():
        pl.semaphore_signal(barrier, inc=1, device_id={"section": s + 1}, device_id_type=MESH)

    sections = (s > 0).astype(jnp.int32) + (s < n_section - 1).astype(jnp.int32)
    pl.semaphore_wait(barrier, n - 1 + sections)

    @pl.when(s == 0)
    def _():
        enter_first(0)

    loop(1, n_dp, lambda k: grads(k).start())

    @pl.when(s == 0)
    def _():
        for m in range(1, micro):
            enter_first(m)

    @pl.when(s > 0)
    def _():
        update()
        merge()
        enter_later(0)

    for m in range(micro):
        project(m)
        if m == 0:

            @pl.when(s == 0)
            def _():
                update()

        if m + 1 < micro:

            @pl.when(s > 0)
            def _(m=m):
                enter_later(m + 1)

        attend(m)
        if m == 0:

            @pl.when(s == 0)
            def _():
                merge()

        leave(m)

    loop(1, n_dp, lambda k: grads(k).wait_send())
    sent_all(3, 0)
    for m in range(micro):
        to_sibling(m).wait_send()
        loop(1, n_dp, lambda k: to_shard(m, k).wait_send())
        loop(1, n_dp, lambda k: forward(m, k).wait_send())
        for kind in range(3):
            sent_all(kind, m)

        @pl.when(s < n_section - 1)
        def _():
            onward(m, jnp.minimum(s + 1, n_section - 1)).wait_send()


def on_device(
    x_in,
    subtree_end,
    norm_gain,
    w_query,
    w_kv,
    w_out,
    a_query,
    b_query,
    a_out,
    b_out,
    grad_a_query,
    grad_b_query,
    grad_a_out,
    grad_b_out,
):
    n_dp, n_section = lax.axis_size("dp"), lax.axis_size("section")
    n = 2 * n_dp
    shard = lax.axis_index(("dp", "tensor"))
    micro, tok, feat = x_in.shape
    width, kv_cols = w_kv.shape[1:]
    rank = a_query.shape[2]
    own = (a_query[0].astype(F32) / n_dp - RATE * grad_a_query[0, 0]).astype(BF16)
    rest = jnp.zeros((width, HD - kv_cols - rank), BF16)
    w_side = jnp.concatenate([w_kv[0], own, rest], axis=1)
    sliced = [
        grad_b_out[0, 0].astype(BF16).reshape(rank, n, feat),
        grad_b_query[0, 0].astype(BF16).reshape(rank, n, HD),
        grad_a_out[0, 0].astype(BF16).T.reshape(rank, n, HD),
    ]
    gradients = jnp.concatenate(sliced, axis=2).transpose(1, 0, 2)
    rows = lax.dynamic_slice_in_dim(a_out[0], shard * HD, HD, 0)
    base = jnp.concatenate([b_out[0], b_query[0], rows.T], axis=1)
    vmem = pl.BlockSpec(memory_space=pltpu.VMEM)
    hbm = pl.BlockSpec(memory_space=pl.ANY)
    dma = pltpu.SemaphoreType.DMA
    extra = feat + 2 * HD
    return pl.pallas_call(
        functools.partial(chain, (n_dp, n_section, kv_cols)),
        out_shape=jax.ShapeDtypeStruct((micro, tok, feat), BF16),
        in_specs=[vmem] * 5 + [hbm] * 3,
        out_specs=vmem,
        scratch_shapes=[
            pltpu.VMEM((width, 2 * HD), BF16),
            pltpu.VMEM((n * HD, feat), BF16),
            pltpu.VMEM((micro, n, tok, feat), BF16),
            pltpu.VMEM((micro, n, 8, HD), F32),
            pltpu.VMEM((micro, tok, feat), BF16),
            pltpu.VMEM((micro, n, tok, HD), BF16),
            pltpu.VMEM((micro, n, tok, HD), BF16),
            pltpu.VMEM((n_dp, rank, extra), BF16),
            pltpu.VMEM((n, rank, HD), BF16),
            pltpu.VMEM((rank, feat), BF16),
            pltpu.VMEM((HD, HD), BF16),
            pltpu.VMEM((tok, 2 * HD), F32),
            pltpu.VMEM((tok, HD), F32),
            dma((3,)),
            dma((micro, n_dp)),
            dma((micro, n_dp)),
            dma((micro, n)),
            dma((micro, n)),
            dma((micro, n)),
            dma((micro, n)),
            dma((micro, n)),
            dma((micro, n)),
            dma((micro, n)),
            dma((n_dp,)),
            dma((n_dp,)),
            dma((n,)),
            dma((n,)),
            dma((micro,)),
            dma((micro,)),
        ],
        compiler_params=pltpu.CompilerParams(
            collective_id=0, has_side_effects=True, vmem_limit_bytes=48 * 2**20
        ),
    )(
        x_in,
        subtree_end[:, None, :],
        norm_gain.astype(F32),
        gradients,
        base,
        w_query[0],
        w_side,
        w_out[0],
    )[None]


def solution(mesh):
    placed = (
        P("groups", None, ("dp", "tensor")),
        P("groups", None),
        P("section", ("dp", "tensor")),
        P("section", None, ("dp", "tensor")),
        P("section", None, ("dp", "tensor")),
        P("section", None, ("dp", "tensor")),
        P("section", None, None),
        P("section", None, ("dp", "tensor")),
        P("section", None, None),
        P("section", None, ("dp", "tensor")),
        P("section", "dp", None, None),
        P("section", "dp", None, None),
        P("section", "dp", None, None),
        P("section", "dp", None, None),
    )
    return jax.shard_map(
        on_device,
        mesh=mesh,
        in_specs=placed,
        out_specs=P("section", "groups", None, ("dp", "tensor")),
        check_vma=False,
    )
```

```python
import functools

import jax
import jax.numpy as jnp
from jax import lax
from jax.experimental import pallas as pl
from jax.experimental.pallas import tpu as pltpu
from jax.sharding import PartitionSpec as P

HD = 128
GROUP = 8
RATE = 0.5
EPS = 1e-05
MESH = pl.DeviceIdType.MESH
F32 = jnp.float32
BF16 = jnp.bfloat16


def chain(
    sizes,
    x_ref,
    ends_ref,
    gain_ref,
    bout_ref,
    bq_ref,
    aout_ref,
    gbq_ref,
    gao_ref,
    gbo_hbm,
    aq_hbm,
    gaq_hbm,
    wq_hbm,
    wkv_hbm,
    wo_hbm,
    out_ref,
    wcat,
    side,
    aq,
    gaq,
    gbo,
    merged,
    blocks,
    squares,
    hidden,
    kvx,
    mix,
    aot,
    gout,
    grecv,
    help_in,
    help_out,
    gown,
    gnext,
    bo,
    bpad,
    acc,
    scaled_q,
    w_sem,
    blk_sems,
    sq_sems,
    kv_sems,
    mix_sems,
    ao_sems,
    g_send,
    g_recv,
    hop_send,
    hop_recv,
    in_send,
    in_recv,
    in_on,
    next_send,
    next_recv,
    next_on,
    hid_send,
    hid_recv,
    gain_sem,
):
    n_dp, n_section, kv_cols = sizes
    n = 2 * n_dp
    micro, tok, feat = x_ref.shape
    rank = bout_ref.shape[0]
    width = n * feat
    last = micro - 1
    d, t, s = lax.axis_index("dp"), lax.axis_index("tensor"), lax.axis_index("section")
    me = 2 * d + t

    def along(k):
        return lax.rem(d + k, n_dp)

    def loop(low, high, body):
        def step(k, carry):
            body(k)
            return carry

        lax.fori_loop(low, high, step, jnp.int32(0))

    def remote(src, dst, send, recv, to):
        return pltpu.make_async_remote_copy(
            src_ref=src,
            dst_ref=dst,
            send_sem=send,
            recv_sem=recv,
            device_id=to,
            device_id_type=MESH,
        )

    loads = (
        lambda: pltpu.make_async_copy(wq_hbm, wcat.at[:, pl.ds(0, HD)], w_sem.at[0]),
        lambda: pltpu.make_async_copy(wkv_hbm, side.at[pl.ds(0, kv_cols)], w_sem.at[1]),
        lambda: pltpu.make_async_copy(wo_hbm, merged, w_sem.at[2]),
        lambda: pltpu.make_async_copy(aq_hbm, aq, w_sem.at[3]),
        lambda: pltpu.make_async_copy(gaq_hbm, gaq, w_sem.at[4]),
        lambda: pltpu.make_async_copy(gbo_hbm, gbo, w_sem.at[5]),
    )

    def of(kind, m):
        buffer, (send, on, recv) = (
            (squares, sq_sems),
            (kvx, kv_sems),
            (mix, mix_sems),
            (aot, ao_sems),
            (blocks, blk_sems),
        )[kind]
        return buffer.at[m], send.at[m], on.at[m], recv.at[m]

    def outward(kind, m, k):
        buffer, send, _, recv = of(kind, m)
        return remote(
            buffer.at[me], buffer.at[me], send.at[k], recv.at[me], {"dp": along(k), "tensor": t}
        )

    def sibling(kind, m):
        buffer, send, _, recv = of(kind, m)
        return remote(buffer.at[me], buffer.at[me], send.at[0], recv.at[me], {"tensor": 1 - t})

    def passed(kind, m, k):
        buffer, _, on, recv = of(kind, m)
        i = 2 * along(k) + t
        return remote(buffer.at[i], buffer.at[i], on.at[k], recv.at[i], {"tensor": 1 - t})

    def landed(kind, m, i):
        buffer, send, _, recv = of(kind, m)
        remote(
            buffer.at[i], buffer.at[i], send.at[0], recv.at[i], {"tensor": 1 - t}
        ).wait_recv()

    def share(kind, m):
        loop(1, n_dp, lambda k: outward(kind, m, k).start())
        sibling(kind, m).start()

    def collect(kind, m, use=None):
        def near(k):
            i = 2 * along(k) + t
            landed(kind, m, i)
            passed(kind, m, k).start()
            if use is not None:
                use(i)

        def far(k):
            i = 2 * along(k) + 1 - t
            landed(kind, m, i)
            if use is not None:
                use(i)

        loop(1, n_dp, near)
        loop(0, n_dp, far)

    def sent(kind, m, wide=True):
        if wide:
            loop(1, n_dp, lambda k: outward(kind, m, k).wait_send())
        sibling(kind, m).wait_send()
        loop(1, n_dp, lambda k: passed(kind, m, k).wait_send())

    def grads(k):
        i = along(k)
        to = {"dp": i, "tensor": t}
        return remote(gout.at[2 * i + t], grecv.at[d], g_send.at[k], g_recv.at[d], to)

    def grads_in(k):
        i = along(k)
        to = {"dp": i, "tensor": t}
        return remote(gout.at[me], grecv.at[i], g_send.at[k], g_recv.at[i], to)

    def give_grads():
        loads[5]().wait()

        def fill(j):
            cols = pl.ds(pl.multiple_of(j * feat, feat), feat)
            heads = pl.ds(pl.multiple_of(j * HD, HD), HD)
            gout[j, :, pl.ds(0, feat)] = gbo[:, cols].astype(BF16)
            gout[j, :, pl.ds(feat, HD)] = gbq_ref[:, heads].astype(BF16)
            gout[j, :, pl.ds(feat + HD, HD)] = gao_ref[:, heads].astype(BF16)

        loop(0, n, fill)
        loop(1, n_dp, lambda k: grads(k).start())

    def join_weights():
        for k in (0, 1, 3, 4):
            loads[k]().wait()
        used = kv_cols + rank
        side[pl.ds(used, HD - used), :] = jnp.zeros((HD - used, width), BF16)

        def part(j):
            cols = pl.ds(pl.multiple_of(j * feat, feat), feat)
            own = aq[:, cols].astype(F32) / n_dp - RATE * gaq[:, cols]
            side[pl.ds(kv_cols, rank), cols] = own.astype(BF16)
            wcat[cols, pl.ds(HD, HD)] = jnp.transpose(side[:, cols])

        loop(0, n, part)

    def hop():
        to = {"section": jnp.minimum(s + 1, n_section - 1)}
        return remote(blocks.at[last, me], help_in.at[d], hop_send, hop_recv, to)

    def help_out_copy(buffer, send, recv, k):
        to = {"dp": along(k), "tensor": t}
        return remote(buffer.at[d], buffer.at[d], send.at[k], recv.at[d], to)

    def help_landed(buffer, send, recv, k):
        i = along(k)
        to = {"dp": i, "tensor": t}
        remote(buffer.at[i], buffer.at[i], send.at[k], recv.at[i], to).wait_recv()

    def help_on(buffer, on, k, section):
        i = along(k)
        row = 2 * i + t
        _, _, _, recv = of(4, last)
        return remote(
            buffer.at[i], blocks.at[last, row], on.at[k], recv.at[row], {"section": section}
        )

    before = jnp.maximum(s - 1, 0)
    after = jnp.minimum(s + 1, n_section - 1)

    def gain_copy():
        return remote(gown, gnext, gain_sem.at[0], gain_sem.at[1], {"section": before})

    def gain_landed():
        remote(gown, gnext, gain_sem.at[0], gain_sem.at[1], {"section": after}).wait_recv()

    def onward(m, to):
        return remote(out_ref.at[m], hidden.at[m], hid_send.at[m], hid_recv.at[m], {"section": to})

    def enter(m):
        wide = hidden[m].astype(F32)
        blocks[m, me] = (wide * gain_ref[...]).astype(BF16)
        if m < last:
            share(4, m)
        else:

            @pl.when(s == 0)
            def _():
                hop().start()

            sibling(4, m).start()
        column = jnp.sum(wide * wide, axis=1, keepdims=True)
        squares[m, me] = jnp.transpose(jnp.broadcast_to(column, (tok, HD)))[:8]
        share(0, m)

    def enter_first(m):
        hidden[m] = x_ref[m]
        enter(m)

    def enter_later(m):
        onward(m, before).wait_recv()
        enter(m)

    def project(m):
        def block(i):
            rows = pl.ds(pl.multiple_of(i * feat, feat), feat)
            acc[...] += jnp.dot(blocks[m, i], wcat[rows, :], preferred_element_type=F32)

        acc[...] = jnp.zeros_like(acc)
        block(me)
        collect(4, m, block)
        collect(0, m)
        total = jnp.sum(squares[m], axis=0)[:1]
        column = jnp.transpose(jnp.broadcast_to(total, (tok, HD)))
        inverse = lax.rsqrt(column / width + EPS)
        kvx[m, me] = (acc[:, HD:] * inverse).astype(BF16)
        share(1, m)
        scaled_q[...] = acc[:, :HD] * inverse

    def update():
        total = gout[me].astype(F32)
        loop(1, n_dp, lambda k: grads_in(k).wait_recv())
        for k in range(1, n_dp):
            total = total + grecv[along(k)].astype(F32)
        heads = pl.ds(pl.multiple_of(me * HD, HD), HD)
        total = RATE * total
        fresh = aout_ref[:, heads].astype(F32) - total[:, feat + HD :]
        aot[0, me] = fresh.astype(BF16)
        share(3, 0)
        bo[...] = (bout_ref[...].astype(F32) - total[:, :feat]).astype(BF16)
        fresh = bq_ref[...].astype(F32) - total[:, feat : feat + HD]
        bpad[...] = jnp.zeros_like(bpad)
        bpad[pl.ds(kv_cols, rank), :] = fresh.astype(BF16)

    def merge():
        loads[2]().wait()
        collect(3, 0)

        def rows_of(j):
            rows = pl.ds(pl.multiple_of(j * HD, HD), HD)
            product = lax.dot_general(
                aot[0, j], bo[...], (((0,), (0,)), ((), ())), preferred_element_type=F32
            )
            merged[rows, :] = (merged[rows, :].astype(F32) + product).astype(BF16)

        loop(0, n, rows_of)

    def attend(m):
        collect(1, m)
        query = scaled_q[...]
        for k in range(n_dp):
            query = query + jnp.dot(kvx[m, 2 * k + t], bpad[...], preferred_element_type=F32)
        query = query.astype(BF16)
        per = HD // kv_cols
        first = me // GROUP * 2 * per
        spot = lax.broadcasted_iota(jnp.int32, (HD, HD), 0)
        lane = lax.broadcasted_iota(jnp.int32, (HD, HD), 1)
        keys = jnp.zeros((tok, HD), F32)
        values = jnp.zeros((tok, HD), F32)
        for i in range(per):
            pick = jnp.where((spot < kv_cols) & (lane == spot + i * kv_cols), 1.0, 0.0).astype(BF16)
            keys = keys + jnp.dot(kvx[m, first + i], pick, preferred_element_type=F32)
            values = values + jnp.dot(kvx[m, first + per + i], pick, preferred_element_type=F32)
        scores = lax.dot_general(
            query, keys.astype(BF16), (((1,), (1,)), ((), ())), preferred_element_type=F32
        ) * HD ** (-0.5)
        here = lax.broadcasted_iota(jnp.int32, (tok, tok), 0)
        there = lax.broadcasted_iota(jnp.int32, (tok, tok), 1)
        visible = (there <= here) & (ends_ref[m] >= here)
        scores = jnp.where(visible, scores, -1e30)
        raised = jnp.exp(scores - jnp.max(scores, axis=-1, keepdims=True))
        portion = (raised / jnp.sum(raised, axis=-1, keepdims=True)).astype(BF16)
        mixed = jnp.dot(portion, values.astype(BF16), preferred_element_type=F32)
        mix[m, me] = mixed.astype(BF16)
        share(2, m)

    def leave(m):
        collect(2, m)
        heads = jnp.concatenate([mix[m, j] for j in range(n)], axis=1)
        total = jnp.dot(heads, merged[...], preferred_element_type=F32)
        out_ref[m] = (hidden[m].astype(F32) + total).astype(BF16)

        @pl.when(s < n_section - 1)
        def _():
            onward(m, after).start()
            if m == last:
                gain_landed()
                help_out[d] = (out_ref[m].astype(F32) * gnext[:1]).astype(BF16)
                loop(1, n_dp, lambda k: help_out_copy(help_out, next_send, next_recv, k).start())

                def relay(k):
                    help_landed(help_out, next_send, next_recv, k)
                    help_on(help_out, next_on, k, after).start()

                loop(1, n_dp, relay)

    for load in loads:
        load().start()
    gown[...] = jnp.broadcast_to(gain_ref[...], gown.shape)
    barrier = pltpu.get_barrier_semaphore()

    def greet(k):
        i = lax.rem(me + k, n)
        to = {"dp": i // 2, "tensor": lax.rem(i, 2)}
        pl.semaphore_signal(barrier, inc=1, device_id=to, device_id_type=MESH)

    loop(1, n, greet)

    @pl.when(s > 0)
    def _():
        pl.semaphore_signal(barrier, inc=1, device_id={"section": s - 1}, device_id_type=MESH)

    @pl.when(s < n_section - 1)
    def _():
        pl.semaphore_signal(barrier, inc=1, device_id={"section": s + 1}, device_id_type=MESH)

    sections = (s > 0).astype(jnp.int32) + (s < n_section - 1).astype(jnp.int32)
    pl.semaphore_wait(barrier, n - 1 + sections)

    @pl.when(s == 0)
    def _():
        for m in range(micro):
            enter_first(m)

    @pl.when(s > 0)
    def _():
        gain_copy().start()

    give_grads()

    @pl.when(s == 1)
    def _():
        remote(blocks.at[last, me], help_in.at[d], hop_send, hop_recv, {"section": 0}).wait_recv()
        loop(1, n_dp, lambda k: help_out_copy(help_in, in_send, in_recv, k).start())

    join_weights()

    @pl.when(s == 1)
    def _():
        def relay(k):
            help_landed(help_in, in_send, in_recv, k)
            help_on(help_in, in_on, k, 0).start()

        loop(1, n_dp, relay)

    @pl.when(s > 0)
    def _():
        update()
        merge()
        enter_later(0)

    for m in range(micro):
        project(m)
        if m == 0:

            @pl.when(s == 0)
            def _():
                update()

        if m + 1 < micro:

            @pl.when(s > 0)
            def _(m=m):
                enter_later(m + 1)

        attend(m)
        if m == 0:

            @pl.when(s == 0)
            def _():
                merge()

        leave(m)

    loop(1, n_dp, lambda k: grads(k).wait_send())
    sent(3, 0)
    for m in range(micro):
        for kind in range(3):
            sent(kind, m)
        sent(4, m, m < last)

    @pl.when(s == 0)
    def _():
        hop().wait_send()

    @pl.when(s == 1)
    def _():
        loop(1, n_dp, lambda k: help_out_copy(help_in, in_send, in_recv, k).wait_send())
        loop(1, n_dp, lambda k: help_on(help_in, in_on, k, 0).wait_send())

    @pl.when(s > 0)
    def _():
        gain_copy().wait_send()

    @pl.when(s < n_section - 1)
    def _():
        for m in range(micro):
            onward(m, after).wait_send()
        loop(1, n_dp, lambda k: help_out_copy(help_out, next_send, next_recv, k).wait_send())
        loop(1, n_dp, lambda k: help_on(help_out, next_on, k, after).wait_send())


def on_device(
    x_in,
    subtree_end,
    norm_gain,
    w_query,
    w_kv,
    w_out,
    a_query,
    b_query,
    a_out,
    b_out,
    grad_a_query,
    grad_b_query,
    grad_a_out,
    grad_b_out,
):
    n_dp, n_section = lax.axis_size("dp"), lax.axis_size("section")
    n = 2 * n_dp
    micro, tok, feat = x_in.shape
    width, kv_cols = w_kv.shape[1:]
    rank = a_query.shape[2]
    vmem = pl.BlockSpec(memory_space=pltpu.VMEM)
    hbm = pl.BlockSpec(memory_space=pl.ANY)
    dma = pltpu.SemaphoreType.DMA
    extra = feat + 2 * HD

    def exchange(count):
        return (dma((count, n_dp)), dma((count, n_dp)), dma((count, n)))

    return pl.pallas_call(
        functools.partial(chain, (n_dp, n_section, kv_cols)),
        out_shape=jax.ShapeDtypeStruct((micro, tok, feat), BF16),
        in_specs=[vmem] * 8 + [hbm] * 6,
        out_specs=vmem,
        scratch_shapes=[
            pltpu.VMEM((width, 2 * HD), BF16),
            pltpu.VMEM((HD, width), BF16),
            pltpu.VMEM((rank, width), BF16),
            pltpu.VMEM((rank, width), F32),
            pltpu.VMEM((rank, width), F32),
            pltpu.VMEM((n * HD, feat), BF16),
            pltpu.VMEM((micro, n, tok, feat), BF16),
            pltpu.VMEM((micro, n, 8, HD), F32),
            pltpu.VMEM((micro, tok, feat), BF16),
            pltpu.VMEM((micro, n, tok, HD), BF16),
            pltpu.VMEM((micro, n, tok, HD), BF16),
            pltpu.VMEM((1, n, rank, HD), BF16),
            pltpu.VMEM((n, rank, extra), BF16),
            pltpu.VMEM((n_dp, rank, extra), BF16),
            pltpu.VMEM((n_dp, tok, feat), BF16),
            pltpu.VMEM((n_dp, tok, feat), BF16),
            pltpu.VMEM((8, feat), F32),
            pltpu.VMEM((8, feat), F32),
            pltpu.VMEM((rank, feat), BF16),
            pltpu.VMEM((HD, HD), BF16),
            pltpu.VMEM((tok, 2 * HD), F32),
            pltpu.VMEM((tok, HD), F32),
            dma((6,)),
            exchange(micro),
            exchange(micro),
            exchange(micro),
            exchange(micro),
            exchange(1),
            dma((n_dp,)),
            dma((n_dp,)),
            dma,
            dma,
            dma((n_dp,)),
            dma((n_dp,)),
            dma((n_dp,)),
            dma((n_dp,)),
            dma((n_dp,)),
            dma((n_dp,)),
            dma((micro,)),
            dma((micro,)),
            dma((2,)),
        ],
        compiler_params=pltpu.CompilerParams(
            collective_id=0, has_side_effects=True, vmem_limit_bytes=48 * 2**20
        ),
    )(
        x_in,
        subtree_end[:, None, :],
        norm_gain.astype(F32),
        b_out[0],
        b_query[0],
        a_out[0].T,
        grad_b_query[0, 0],
        grad_a_out[0, 0].T,
        grad_b_out[0, 0],
        a_query[0].T,
        grad_a_query[0, 0].T,
        w_query[0],
        w_kv[0].T,
        w_out[0],
    )[None]


def solution(mesh):
    placed = (
        P("groups", None, ("dp", "tensor")),
        P("groups", None),
        P("section", ("dp", "tensor")),
        P("section", None, ("dp", "tensor")),
        P("section", None, ("dp", "tensor")),
        P("section", None, ("dp", "tensor")),
        P("section", None, None),
        P("section", None, ("dp", "tensor")),
        P("section", None, None),
        P("section", None, ("dp", "tensor")),
        P("section", "dp", None, None),
        P("section", "dp", None, None),
        P("section", "dp", None, None),
        P("section", "dp", None, None),
    )
    return jax.shard_map(
        on_device,
        mesh=mesh,
        in_specs=placed,
        out_specs=P("section", "groups", None, ("dp", "tensor")),
        check_vma=False,
    )
```

```python
import functools

import jax
import jax.numpy as jnp
from jax import lax
from jax.experimental import pallas as pl
from jax.experimental.pallas import tpu as pltpu
from jax.sharding import PartitionSpec as P

HD = 128
GROUP = 8
RATE = 0.5
EPS = 1e-05
MESH = pl.DeviceIdType.MESH
F32 = jnp.float32
BF16 = jnp.bfloat16


def chain(
    sizes,
    ends_ref,
    gain_ref,
    x_hbm,
    bout_hbm,
    bq_hbm,
    aout_hbm,
    gbq_hbm,
    gao_hbm,
    gbo_hbm,
    aq_hbm,
    gaq_hbm,
    wq_hbm,
    wkv_hbm,
    wo_hbm,
    out_ref,
    wcat,
    side,
    aq,
    gaq,
    gbo,
    bout_ref,
    bq_ref,
    aout_ref,
    gbq_ref,
    gao_ref,
    merged,
    blocks,
    squares,
    hidden,
    kvx,
    mix,
    aot,
    gout,
    grecv,
    halves,
    help_in,
    help_out,
    gown,
    gnext,
    bo,
    bpad,
    acc,
    scaled_q,
    w_sem,
    blk_sems,
    sq_sems,
    kv_sems,
    mix_sems,
    ao_sems,
    g_send,
    g_recv,
    hop_send,
    hop_recv,
    in_send,
    in_recv,
    in_on,
    next_send,
    next_recv,
    next_on,
    hid_send,
    hid_recv,
    gain_sem,
    half_recv,
    low_send,
    y_sem,
    x_sem,
):
    n_dp, n_section, kv_cols = sizes
    n = 2 * n_dp
    micro, tok, feat = hidden.shape
    rank = bout_ref.shape[0]
    width = n * feat
    last = micro - 1
    d, t, s = lax.axis_index("dp"), lax.axis_index("tensor"), lax.axis_index("section")
    y = lax.axis_index("groups")
    me = 2 * d + t
    cut = tok // 2
    half = rank // 2

    def along(k):
        return lax.rem(d + k, n_dp)

    def loop(low, high, body):
        def step(k, carry):
            body(k)
            return carry

        lax.fori_loop(low, high, step, jnp.int32(0))

    def remote(src, dst, send, recv, to):
        return pltpu.make_async_remote_copy(
            src_ref=src,
            dst_ref=dst,
            send_sem=send,
            recv_sem=recv,
            device_id=to,
            device_id_type=MESH,
        )

    loads = (
        lambda: pltpu.make_async_copy(wq_hbm, wcat.at[:, pl.ds(0, HD)], w_sem.at[0]),
        lambda: pltpu.make_async_copy(wkv_hbm, side.at[pl.ds(0, kv_cols)], w_sem.at[1]),
        lambda: pltpu.make_async_copy(wo_hbm, merged, w_sem.at[2]),
        lambda: pltpu.make_async_copy(aq_hbm, aq, w_sem.at[3]),
        lambda: pltpu.make_async_copy(gaq_hbm, gaq, w_sem.at[4]),
        lambda: pltpu.make_async_copy(gbo_hbm, gbo, w_sem.at[5]),
        lambda: pltpu.make_async_copy(gbq_hbm, gbq_ref, w_sem.at[6]),
        lambda: pltpu.make_async_copy(gao_hbm, gao_ref, w_sem.at[7]),
        lambda: pltpu.make_async_copy(bout_hbm, bout_ref, w_sem.at[8]),
        lambda: pltpu.make_async_copy(bq_hbm, bq_ref, w_sem.at[9]),
        lambda: pltpu.make_async_copy(aout_hbm, aout_ref, w_sem.at[10]),
    )

    def of(kind, m):
        buffer, (send, on, recv) = (
            (squares, sq_sems),
            (kvx, kv_sems),
            (mix, mix_sems),
            (aot, ao_sems),
            (blocks, blk_sems),
        )[kind]
        return buffer.at[m], send.at[m], on.at[m], recv.at[m]

    def outward(kind, m, k):
        buffer, send, _, recv = of(kind, m)
        return remote(
            buffer.at[me], buffer.at[me], send.at[k], recv.at[me], {"dp": along(k), "tensor": t}
        )

    def sibling(kind, m):
        buffer, send, _, recv = of(kind, m)
        return remote(buffer.at[me], buffer.at[me], send.at[0], recv.at[me], {"tensor": 1 - t})

    def passed(kind, m, k):
        buffer, _, on, recv = of(kind, m)
        i = 2 * along(k) + t
        return remote(buffer.at[i], buffer.at[i], on.at[k], recv.at[i], {"tensor": 1 - t})

    def landed(kind, m, i):
        buffer, send, _, recv = of(kind, m)
        remote(
            buffer.at[i], buffer.at[i], send.at[0], recv.at[i], {"tensor": 1 - t}
        ).wait_recv()

    def share(kind, m):
        loop(1, n_dp, lambda k: outward(kind, m, k).start())
        sibling(kind, m).start()

    def collect(kind, m, use=None):
        def near(k):
            i = 2 * along(k) + t
            if kind == 4 and m == last:
                for part in range(2):
                    rows = blocks.at[m, i, pl.ds(part * cut, cut)]
                    sem = half_recv.at[part, i]
                    remote(rows, rows, low_send.at[k], sem, {"tensor": 1 - t}).wait_recv()
            else:
                landed(kind, m, i)
            passed(kind, m, k).start()
            if use is not None:
                use(i)

        def far(k):
            i = 2 * along(k) + 1 - t
            landed(kind, m, i)
            if use is not None:
                use(i)

        loop(1, n_dp, near)
        loop(0, n_dp, far)

    def sent(kind, m, wide=True):
        if wide:
            loop(1, n_dp, lambda k: outward(kind, m, k).wait_send())
        sibling(kind, m).wait_send()
        loop(1, n_dp, lambda k: passed(kind, m, k).wait_send())

    def grads(k):
        i = along(k)
        to = {"dp": i, "tensor": t}
        rows = pl.ds(pl.multiple_of(y * half, half), half)
        return remote(
            gout.at[2 * i + t, rows], grecv.at[d, rows], g_send.at[k], g_recv.at[d], to
        )

    def grads_in(k):
        i = along(k)
        to = {"dp": i, "tensor": t}
        rows = pl.ds(pl.multiple_of(y * half, half), half)
        return remote(gout.at[me, rows], grecv.at[i, rows], g_send.at[k], g_recv.at[i], to)

    def sums(k):
        return remote(halves.at[k], halves.at[k], y_sem.at[0], y_sem.at[1 + k], {"groups": 1 - y})

    def give_grads():
        for k in (5, 6, 7):
            loads[k]().wait()

        def fill(j):
            cols = pl.ds(pl.multiple_of(j * feat, feat), feat)
            heads = pl.ds(pl.multiple_of(j * HD, HD), HD)
            gout[j, :, pl.ds(0, feat)] = gbo[:, cols].astype(BF16)
            gout[j, :, pl.ds(feat, HD)] = gbq_ref[:, heads].astype(BF16)
            gout[j, :, pl.ds(feat + HD, HD)] = gao_ref[:, heads].astype(BF16)

        loop(0, n, fill)
        loop(1, n_dp, lambda k: grads(k).start())

    def join_weights():
        for k in (0, 1, 3, 4):
            loads[k]().wait()
        used = kv_cols + rank
        side[pl.ds(used, HD - used), :] = jnp.zeros((HD - used, width), BF16)

        def part(j):
            cols = pl.ds(pl.multiple_of(j * feat, feat), feat)
            own = aq[:, cols].astype(F32) / n_dp - RATE * gaq[:, cols]
            side[pl.ds(kv_cols, rank), cols] = own.astype(BF16)
            wcat[cols, pl.ds(HD, HD)] = jnp.transpose(side[:, cols])

        loop(0, n, part)

    def hop():
        to = {"section": jnp.minimum(s + 1, n_section - 1)}
        return remote(blocks.at[last, me], help_in.at[d], hop_send, hop_recv, to)

    def help_copy(buffer, send, recv, k, part):
        to = {"dp": along(k), "tensor": t}
        rows = buffer.at[d, pl.ds(part * cut, cut)]
        return remote(rows, rows, send.at[part, k], recv.at[part, d], to)

    def help_landed(buffer, send, recv, k, part):
        i = along(k)
        to = {"dp": i, "tensor": t}
        rows = buffer.at[i, pl.ds(part * cut, cut)]
        remote(rows, rows, send.at[part, k], recv.at[part, i], to).wait_recv()

    def help_on(buffer, on, k, part, section):
        i = along(k)
        row = 2 * i + t
        rows = pl.ds(part * cut, cut)
        return remote(
            buffer.at[i, rows],
            blocks.at[last, row, rows],
            on.at[part, k],
            half_recv.at[part, row],
            {"section": section},
        )

    def lower(k):
        rows = blocks.at[last, me, pl.ds(cut, cut)]
        to = {"dp": along(k), "tensor": t}
        return remote(rows, rows, low_send.at[k], half_recv.at[1, me], to)

    before = jnp.maximum(s - 1, 0)
    after = jnp.minimum(s + 1, n_section - 1)

    def gain_copy():
        return remote(gown, gnext, gain_sem.at[0], gain_sem.at[1], {"section": before})

    def gain_landed():
        remote(gown, gnext, gain_sem.at[0], gain_sem.at[1], {"section": after}).wait_recv()

    def onward(m, to):
        return remote(out_ref.at[m], hidden.at[m], hid_send.at[m], hid_recv.at[m], {"section": to})

    def enter(m):
        wide = hidden[m].astype(F32)
        blocks[m, me] = (wide * gown[:1]).astype(BF16)
        if m < last:
            share(4, m)
        else:

            @pl.when(s == 0)
            def _():
                hop().start()

            @pl.when(s > 0)
            def _():
                loop(1, n_dp, lambda k: lower(k).start())

            sibling(4, m).start()
        column = jnp.sum(wide * wide, axis=1, keepdims=True)
        squares[m, me] = jnp.transpose(jnp.broadcast_to(column, (tok, HD)))[:8]
        share(0, m)

    def entering(m):
        return pltpu.make_async_copy(x_hbm.at[m], hidden.at[m], x_sem.at[m])

    def enter_first(m):
        entering(m).wait()
        enter(m)

    def enter_later(m):
        onward(m, before).wait_recv()
        enter(m)

    def project(m):
        def block(i):
            rows = pl.ds(pl.multiple_of(i * feat, feat), feat)
            acc[...] += jnp.dot(blocks[m, i], wcat[rows, :], preferred_element_type=F32)

        acc[...] = jnp.zeros_like(acc)
        block(me)
        collect(4, m, block)
        collect(0, m)
        total = jnp.sum(squares[m], axis=0)[:1]
        column = jnp.transpose(jnp.broadcast_to(total, (tok, HD)))
        inverse = lax.rsqrt(column / width + EPS)
        kvx[m, me] = (acc[:, HD:] * inverse).astype(BF16)
        share(1, m)
        scaled_q[...] = acc[:, :HD] * inverse

    def update():
        rows = pl.ds(pl.multiple_of(y * half, half), half)
        total = gout[me, rows].astype(F32)
        loop(1, n_dp, lambda k: grads_in(k).wait_recv())
        for k in range(1, n_dp):
            total = total + grecv[along(k), rows].astype(F32)
        halves[y] = total.astype(BF16)
        sums(y).start()
        for k in (8, 9, 10):
            loads[k]().wait()
        sums(1 - y).wait_recv()
        total = jnp.concatenate([halves[0], halves[1]], axis=0).astype(F32)
        heads = pl.ds(pl.multiple_of(me * HD, HD), HD)
        total = RATE * total
        fresh = aout_ref[:, heads].astype(F32) - total[:, feat + HD :]
        aot[0, me] = fresh.astype(BF16)
        share(3, 0)
        bo[...] = (bout_ref[...].astype(F32) - total[:, :feat]).astype(BF16)
        fresh = bq_ref[...].astype(F32) - total[:, feat : feat + HD]
        bpad[...] = jnp.zeros_like(bpad)
        bpad[pl.ds(kv_cols, rank), :] = fresh.astype(BF16)

    def merge():
        loads[2]().wait()
        collect(3, 0)

        def rows_of(j):
            rows = pl.ds(pl.multiple_of(j * HD, HD), HD)
            product = lax.dot_general(
                aot[0, j], bo[...], (((0,), (0,)), ((), ())), preferred_element_type=F32
            )
            merged[rows, :] = (merged[rows, :].astype(F32) + product).astype(BF16)

        loop(0, n, rows_of)

    def attend(m):
        collect(1, m)
        query = scaled_q[...]
        for k in range(n_dp):
            query = query + jnp.dot(kvx[m, 2 * k + t], bpad[...], preferred_element_type=F32)
        query = query.astype(BF16)
        per = HD // kv_cols
        first = me // GROUP * 2 * per
        spot = lax.broadcasted_iota(jnp.int32, (HD, HD), 0)
        lane = lax.broadcasted_iota(jnp.int32, (HD, HD), 1)
        keys = jnp.zeros((tok, HD), F32)
        values = jnp.zeros((tok, HD), F32)
        for i in range(per):
            pick = jnp.where((spot < kv_cols) & (lane == spot + i * kv_cols), 1.0, 0.0).astype(BF16)
            keys = keys + jnp.dot(kvx[m, first + i], pick, preferred_element_type=F32)
            values = values + jnp.dot(kvx[m, first + per + i], pick, preferred_element_type=F32)
        scores = lax.dot_general(
            query, keys.astype(BF16), (((1,), (1,)), ((), ())), preferred_element_type=F32
        ) * HD ** (-0.5)
        here = lax.broadcasted_iota(jnp.int32, (tok, tok), 0)
        there = lax.broadcasted_iota(jnp.int32, (tok, tok), 1)
        visible = (there <= here) & (ends_ref[m] >= here)
        scores = jnp.where(visible, scores, -1e30)
        raised = jnp.exp(scores - jnp.max(scores, axis=-1, keepdims=True))
        portion = (raised / jnp.sum(raised, axis=-1, keepdims=True)).astype(BF16)
        mixed = jnp.dot(portion, values.astype(BF16), preferred_element_type=F32)
        mix[m, me] = mixed.astype(BF16)
        share(2, m)

    def leave(m):
        collect(2, m)
        heads = jnp.concatenate([mix[m, j] for j in range(n)], axis=1)
        total = jnp.dot(heads, merged[...], preferred_element_type=F32)
        out_ref[m] = (hidden[m].astype(F32) + total).astype(BF16)

        @pl.when(s < n_section - 1)
        def _():
            onward(m, after).start()
            if m == last:
                gain_landed()
                upper = out_ref[m, pl.ds(0, cut), :].astype(F32)
                help_out[d, pl.ds(0, cut), :] = (upper * gnext[:1]).astype(BF16)
                loop(1, n_dp, lambda k: help_copy(help_out, next_send, next_recv, k, 0).start())

                def relay(k):
                    help_landed(help_out, next_send, next_recv, k, 0)
                    help_on(help_out, next_on, k, 0, after).start()

                loop(1, n_dp, relay)

    @pl.when(s == 0)
    def _():
        for m in range(micro):
            entering(m).start()

    for k in (5, 6, 7, 4, 3, 1, 0, 2, 8, 9, 10):
        loads[k]().start()
    gown[...] = jnp.broadcast_to(gain_ref[...].astype(F32), gown.shape)
    barrier = pltpu.get_barrier_semaphore()

    def greet(k):
        i = lax.rem(me + k, n)
        to = {"dp": i // 2, "tensor": lax.rem(i, 2)}
        pl.semaphore_signal(barrier, inc=1, device_id=to, device_id_type=MESH)

    loop(1, n, greet)
    pl.semaphore_signal(barrier, inc=1, device_id={"groups": 1 - y}, device_id_type=MESH)

    @pl.when(s > 0)
    def _():
        pl.semaphore_signal(barrier, inc=1, device_id={"section": s - 1}, device_id_type=MESH)

    @pl.when(s < n_section - 1)
    def _():
        pl.semaphore_signal(barrier, inc=1, device_id={"section": s + 1}, device_id_type=MESH)

    sections = (s > 0).astype(jnp.int32) + (s < n_section - 1).astype(jnp.int32)
    pl.semaphore_wait(barrier, n + sections)

    @pl.when(s == 0)
    def _():
        for m in range(micro):
            enter_first(m)

    @pl.when(s > 0)
    def _():
        gain_copy().start()

    @pl.when(s == 1)
    def _():
        remote(blocks.at[last, me], help_in.at[d], hop_send, hop_recv, {"section": 0}).wait_recv()
        for part in range(2):
            loop(1, n_dp, lambda k: help_copy(help_in, in_send, in_recv, k, part).start())

    give_grads()
    join_weights()

    @pl.when(s == 1)
    def _():
        for part in range(2):

            def relay(k):
                help_landed(help_in, in_send, in_recv, k, part)
                help_on(help_in, in_on, k, part, 0).start()

            loop(1, n_dp, relay)

    @pl.when(s > 0)
    def _():
        enter_later(0)
        update()
        merge()

    for m in range(micro):
        project(m)
        if m == 0:

            @pl.when(s == 0)
            def _():
                update()

        if m + 1 < micro:

            @pl.when(s > 0)
            def _(m=m):
                enter_later(m + 1)

        attend(m)
        if m == 0:

            @pl.when(s == 0)
            def _():
                merge()

        leave(m)

    loop(1, n_dp, lambda k: grads(k).wait_send())
    sums(y).wait_send()
    sent(3, 0)
    for m in range(micro):
        for kind in range(3):
            sent(kind, m)
        sent(4, m, m < last)

    @pl.when(s == 0)
    def _():
        hop().wait_send()

    @pl.when(s == 1)
    def _():
        for part in range(2):
            loop(1, n_dp, lambda k: help_copy(help_in, in_send, in_recv, k, part).wait_send())
            loop(1, n_dp, lambda k: help_on(help_in, in_on, k, part, 0).wait_send())

    @pl.when(s > 0)
    def _():
        gain_copy().wait_send()
        loop(1, n_dp, lambda k: lower(k).wait_send())

    @pl.when(s < n_section - 1)
    def _():
        for m in range(micro):
            onward(m, after).wait_send()
        loop(1, n_dp, lambda k: help_copy(help_out, next_send, next_recv, k, 0).wait_send())
        loop(1, n_dp, lambda k: help_on(help_out, next_on, k, 0, after).wait_send())


def on_device(
    x_in,
    subtree_end,
    norm_gain,
    w_query,
    w_kv,
    w_out,
    a_query,
    b_query,
    a_out,
    b_out,
    grad_a_query,
    grad_b_query,
    grad_a_out,
    grad_b_out,
):
    n_dp, n_section = lax.axis_size("dp"), lax.axis_size("section")
    n = 2 * n_dp
    micro, tok, feat = x_in.shape
    width, kv_cols = w_kv.shape[1:]
    rank = a_query.shape[2]
    vmem = pl.BlockSpec(memory_space=pltpu.VMEM)
    hbm = pl.BlockSpec(memory_space=pltpu.HBM)
    dma = pltpu.SemaphoreType.DMA
    extra = feat + 2 * HD

    def exchange(count):
        return (dma((count, n_dp)), dma((count, n_dp)), dma((count, n)))

    return pl.pallas_call(
        functools.partial(chain, (n_dp, n_section, kv_cols)),
        out_shape=jax.ShapeDtypeStruct((micro, tok, feat), BF16),
        in_specs=[vmem] * 2 + [hbm] * 12,
        out_specs=vmem,
        scratch_shapes=[
            pltpu.VMEM((width, 2 * HD), BF16),
            pltpu.VMEM((HD, width), BF16),
            pltpu.VMEM((rank, width), BF16),
            pltpu.VMEM((rank, width), F32),
            pltpu.VMEM((rank, width), F32),
            pltpu.VMEM((rank, feat), BF16),
            pltpu.VMEM((rank, HD), BF16),
            pltpu.VMEM((rank, n * HD), BF16),
            pltpu.VMEM((rank, n * HD), F32),
            pltpu.VMEM((rank, n * HD), F32),
            pltpu.VMEM((n * HD, feat), BF16),
            pltpu.VMEM((micro, n, tok, feat), BF16),
            pltpu.VMEM((micro, n, 8, HD), F32),
            pltpu.VMEM((micro, tok, feat), BF16),
            pltpu.VMEM((micro, n, tok, HD), BF16),
            pltpu.VMEM((micro, n, tok, HD), BF16),
            pltpu.VMEM((1, n, rank, HD), BF16),
            pltpu.VMEM((n, rank, extra), BF16),
            pltpu.VMEM((n_dp, rank, extra), BF16),
            pltpu.VMEM((2, rank // 2, extra), BF16),
            pltpu.VMEM((n_dp, tok, feat), BF16),
            pltpu.VMEM((n_dp, tok, feat), BF16),
            pltpu.VMEM((8, feat), F32),
            pltpu.VMEM((8, feat), F32),
            pltpu.VMEM((rank, feat), BF16),
            pltpu.VMEM((HD, HD), BF16),
            pltpu.VMEM((tok, 2 * HD), F32),
            pltpu.VMEM((tok, HD), F32),
            dma((11,)),
            exchange(micro),
            exchange(micro),
            exchange(micro),
            exchange(micro),
            exchange(1),
            dma((n_dp,)),
            dma((n_dp,)),
            dma,
            dma,
            dma((2, n_dp)),
            dma((2, n_dp)),
            dma((2, n_dp)),
            dma((2, n_dp)),
            dma((2, n_dp)),
            dma((2, n_dp)),
            dma((micro,)),
            dma((micro,)),
            dma((2,)),
            dma((2, n)),
            dma((n_dp,)),
            dma((3,)),
            dma((micro,)),
        ],
        compiler_params=pltpu.CompilerParams(
            collective_id=0, has_side_effects=True, vmem_limit_bytes=48 * 2**20
        ),
    )(
        subtree_end[:, None, :],
        norm_gain,
        x_in,
        b_out[0],
        b_query[0],
        a_out[0].T,
        grad_b_query[0, 0],
        grad_a_out[0, 0].T,
        grad_b_out[0, 0],
        a_query[0].T,
        grad_a_query[0, 0].T,
        w_query[0],
        w_kv[0].T,
        w_out[0],
    )[None]


def solution(mesh):
    placed = (
        P("groups", None, ("dp", "tensor")),
        P("groups", None),
        P("section", ("dp", "tensor")),
        P("section", None, ("dp", "tensor")),
        P("section", None, ("dp", "tensor")),
        P("section", None, ("dp", "tensor")),
        P("section", None, None),
        P("section", None, ("dp", "tensor")),
        P("section", None, None),
        P("section", None, ("dp", "tensor")),
        P("section", "dp", None, None),
        P("section", "dp", None, None),
        P("section", "dp", None, None),
        P("section", "dp", None, None),
    )
    return jax.shard_map(
        on_device,
        mesh=mesh,
        in_specs=placed,
        out_specs=P("section", "groups", None, ("dp", "tensor")),
        check_vma=False,
    )
```

```python
import functools

import jax
import jax.numpy as jnp
from jax import lax
from jax.experimental import pallas as pl
from jax.experimental.pallas import tpu as pltpu
from jax.sharding import PartitionSpec as P

HD = 128
GROUP = 8
RATE = 0.5
EPS = 1e-05
MESH = pl.DeviceIdType.MESH
F32 = jnp.float32
BF16 = jnp.bfloat16


def chain(
    sizes,
    ends_ref,
    gain_ref,
    x_hbm,
    bout_hbm,
    bq_hbm,
    aout_hbm,
    gbq_hbm,
    gao_hbm,
    gbo_hbm,
    aq_hbm,
    gaq_hbm,
    wq_hbm,
    wkv_hbm,
    wo_hbm,
    out_ref,
    wcat,
    side,
    aq,
    gaq,
    gbo,
    bout_ref,
    bq_ref,
    aout_ref,
    gbq_ref,
    gao_ref,
    merged,
    blocks,
    squares,
    hidden,
    kvx,
    mix,
    aot,
    gout,
    grecv,
    halves,
    help_in,
    help_out,
    gown,
    gnext,
    bo,
    bpad,
    acc,
    scaled_q,
    w_sem,
    blk_sems,
    sq_sems,
    kv_sems,
    mix_sems,
    ao_sems,
    g_send,
    g_recv,
    hop_send,
    hop_recv,
    in_send,
    in_recv,
    in_on,
    next_send,
    next_recv,
    next_on,
    hid_send,
    hid_recv,
    gain_sem,
    half_recv,
    low_send,
    y_sem,
    x_sem,
):
    n_dp, n_section, kv_cols = sizes
    n = 2 * n_dp
    micro, tok, feat = hidden.shape
    rank = bout_ref.shape[0]
    width = n * feat
    last = micro - 1
    d, t, s = lax.axis_index("dp"), lax.axis_index("tensor"), lax.axis_index("section")
    y = lax.axis_index("groups")
    me = 2 * d + t
    cut = tok // 2
    half = rank // 2

    def along(k):
        return lax.rem(d + k, n_dp)

    def loop(low, high, body):
        def step(k, carry):
            body(k)
            return carry

        lax.fori_loop(low, high, step, jnp.int32(0))

    def remote(src, dst, send, recv, to):
        return pltpu.make_async_remote_copy(
            src_ref=src,
            dst_ref=dst,
            send_sem=send,
            recv_sem=recv,
            device_id=to,
            device_id_type=MESH,
        )

    loads = (
        lambda: pltpu.make_async_copy(wq_hbm, wcat.at[:, pl.ds(0, HD)], w_sem.at[0]),
        lambda: pltpu.make_async_copy(wkv_hbm, side.at[pl.ds(0, kv_cols)], w_sem.at[1]),
        lambda: pltpu.make_async_copy(wo_hbm, merged, w_sem.at[2]),
        lambda: pltpu.make_async_copy(aq_hbm, aq, w_sem.at[3]),
        lambda: pltpu.make_async_copy(gaq_hbm, gaq, w_sem.at[4]),
        lambda: pltpu.make_async_copy(gbo_hbm, gbo, w_sem.at[5]),
        lambda: pltpu.make_async_copy(gbq_hbm, gbq_ref, w_sem.at[6]),
        lambda: pltpu.make_async_copy(gao_hbm, gao_ref, w_sem.at[7]),
        lambda: pltpu.make_async_copy(bout_hbm, bout_ref, w_sem.at[8]),
        lambda: pltpu.make_async_copy(bq_hbm, bq_ref, w_sem.at[9]),
        lambda: pltpu.make_async_copy(aout_hbm, aout_ref, w_sem.at[10]),
    )

    def of(kind, m):
        buffer, (send, on, recv) = (
            (squares, sq_sems),
            (kvx, kv_sems),
            (mix, mix_sems),
            (aot, ao_sems),
            (blocks, blk_sems),
        )[kind]
        return buffer.at[m], send.at[m], on.at[m], recv.at[m]

    def outward(kind, m, k):
        buffer, send, _, recv = of(kind, m)
        return remote(
            buffer.at[me], buffer.at[me], send.at[k], recv.at[me], {"dp": along(k), "tensor": t}
        )

    def sibling(kind, m):
        buffer, send, _, recv = of(kind, m)
        return remote(buffer.at[me], buffer.at[me], send.at[0], recv.at[me], {"tensor": 1 - t})

    def passed(kind, m, k):
        buffer, _, on, recv = of(kind, m)
        i = 2 * along(k) + t
        return remote(buffer.at[i], buffer.at[i], on.at[k], recv.at[i], {"tensor": 1 - t})

    def landed(kind, m, i):
        buffer, send, _, recv = of(kind, m)
        remote(
            buffer.at[i], buffer.at[i], send.at[0], recv.at[i], {"tensor": 1 - t}
        ).wait_recv()

    def share(kind, m):
        loop(1, n_dp, lambda k: outward(kind, m, k).start())
        sibling(kind, m).start()

    def collect(kind, m, use=None):
        def near(k):
            i = 2 * along(k) + t
            if kind == 4 and m == last:
                for part in range(2):
                    rows = blocks.at[m, i, pl.ds(part * cut, cut)]
                    sem = half_recv.at[part, i]
                    remote(rows, rows, low_send.at[k], sem, {"tensor": 1 - t}).wait_recv()
            else:
                landed(kind, m, i)
            passed(kind, m, k).start()
            if use is not None:
                use(i)

        def far(k):
            i = 2 * along(k) + 1 - t
            landed(kind, m, i)
            if use is not None:
                use(i)

        loop(1, n_dp, near)
        loop(0, n_dp, far)

    def sent(kind, m, wide=True):
        if wide:
            loop(1, n_dp, lambda k: outward(kind, m, k).wait_send())
        sibling(kind, m).wait_send()
        loop(1, n_dp, lambda k: passed(kind, m, k).wait_send())

    def grads(k):
        i = along(k)
        to = {"dp": i, "tensor": t}
        rows = pl.ds(pl.multiple_of(y * half, half), half)
        return remote(
            gout.at[2 * i + t, rows], grecv.at[d, rows], g_send.at[k], g_recv.at[d], to
        )

    def grads_in(k):
        i = along(k)
        to = {"dp": i, "tensor": t}
        rows = pl.ds(pl.multiple_of(y * half, half), half)
        return remote(gout.at[me, rows], grecv.at[i, rows], g_send.at[k], g_recv.at[i], to)

    def sums(k):
        return remote(halves.at[k], halves.at[k], y_sem.at[0], y_sem.at[1 + k], {"groups": 1 - y})

    def give_grads():
        for k in (5, 6, 7):
            loads[k]().wait()

        def fill(j):
            cols = pl.ds(pl.multiple_of(j * feat, feat), feat)
            heads = pl.ds(pl.multiple_of(j * HD, HD), HD)
            gout[j, :, pl.ds(0, feat)] = gbo[:, cols].astype(BF16)
            gout[j, :, pl.ds(feat, HD)] = gbq_ref[:, heads].astype(BF16)
            gout[j, :, pl.ds(feat + HD, HD)] = gao_ref[:, heads].astype(BF16)

        loop(0, n, fill)
        loop(1, n_dp, lambda k: grads(k).start())

    def join_weights():
        for k in (0, 1, 3, 4):
            loads[k]().wait()
        used = kv_cols + rank
        side[pl.ds(used, HD - used), :] = jnp.zeros((HD - used, width), BF16)

        def part(j):
            cols = pl.ds(pl.multiple_of(j * feat, feat), feat)
            own = aq[:, cols].astype(F32) / n_dp - RATE * gaq[:, cols]
            side[pl.ds(kv_cols, rank), cols] = own.astype(BF16)
            wcat[cols, pl.ds(HD, HD)] = jnp.transpose(side[:, cols])

        loop(0, n, part)

    def hop():
        to = {"section": jnp.minimum(s + 1, n_section - 1)}
        return remote(blocks.at[last, me], help_in.at[d], hop_send, hop_recv, to)

    def help_copy(buffer, send, recv, k, part):
        to = {"dp": along(k), "tensor": t}
        rows = buffer.at[d, pl.ds(part * cut, cut)]
        return remote(rows, rows, send.at[part, k], recv.at[part, d], to)

    def help_landed(buffer, send, recv, k, part):
        i = along(k)
        to = {"dp": i, "tensor": t}
        rows = buffer.at[i, pl.ds(part * cut, cut)]
        remote(rows, rows, send.at[part, k], recv.at[part, i], to).wait_recv()

    def help_on(buffer, on, k, part, section):
        i = along(k)
        row = 2 * i + t
        rows = pl.ds(part * cut, cut)
        return remote(
            buffer.at[i, rows],
            blocks.at[last, row, rows],
            on.at[part, k],
            half_recv.at[part, row],
            {"section": section},
        )

    def lower(k):
        rows = blocks.at[last, me, pl.ds(cut, cut)]
        to = {"dp": along(k), "tensor": t}
        return remote(rows, rows, low_send.at[k], half_recv.at[1, me], to)

    before = jnp.maximum(s - 1, 0)
    after = jnp.minimum(s + 1, n_section - 1)

    def gain_copy():
        return remote(gown, gnext, gain_sem.at[0], gain_sem.at[1], {"section": before})

    def gain_landed():
        remote(gown, gnext, gain_sem.at[0], gain_sem.at[1], {"section": after}).wait_recv()

    def onward(m, to):
        return remote(out_ref.at[m], hidden.at[m], hid_send.at[m], hid_recv.at[m], {"section": to})

    def enter(m):
        wide = hidden[m].astype(F32)
        blocks[m, me] = (wide * gown[:1]).astype(BF16)
        if m < last:
            share(4, m)
        else:

            @pl.when(s == 0)
            def _():
                hop().start()

            @pl.when(s > 0)
            def _():
                loop(1, n_dp, lambda k: lower(k).start())

            sibling(4, m).start()
        column = jnp.sum(wide * wide, axis=1, keepdims=True)
        squares[m, me] = jnp.transpose(jnp.broadcast_to(column, (tok, HD)))[:8]
        share(0, m)

    def entering(m):
        return pltpu.make_async_copy(x_hbm.at[m], hidden.at[m], x_sem.at[m])

    def enter_first(m):
        entering(m).wait()
        enter(m)

    def enter_later(m):
        onward(m, before).wait_recv()
        enter(m)

    def project(m):
        def block(i):
            rows = pl.ds(pl.multiple_of(i * feat, feat), feat)
            acc[...] += jnp.dot(blocks[m, i], wcat[rows, :], preferred_element_type=F32)

        acc[...] = jnp.zeros_like(acc)
        block(me)
        collect(4, m, block)
        collect(0, m)
        total = jnp.sum(squares[m], axis=0)[:1]
        column = jnp.transpose(jnp.broadcast_to(total, (tok, HD)))
        inverse = lax.rsqrt(column / width + EPS)
        kvx[m, me] = (acc[:, HD:] * inverse).astype(BF16)
        share(1, m)
        scaled_q[...] = acc[:, :HD] * inverse

    def update():
        rows = pl.ds(pl.multiple_of(y * half, half), half)
        total = gout[me, rows].astype(F32)
        loop(1, n_dp, lambda k: grads_in(k).wait_recv())
        for k in range(1, n_dp):
            total = total + grecv[along(k), rows].astype(F32)
        halves[y] = total.astype(BF16)
        sums(y).start()
        for k in (8, 9, 10):
            loads[k]().wait()
        sums(1 - y).wait_recv()
        total = jnp.concatenate([halves[0], halves[1]], axis=0).astype(F32)
        heads = pl.ds(pl.multiple_of(me * HD, HD), HD)
        total = RATE * total
        fresh = aout_ref[:, heads].astype(F32) - total[:, feat + HD :]
        aot[0, me] = fresh.astype(BF16)
        share(3, 0)
        bo[...] = (bout_ref[...].astype(F32) - total[:, :feat]).astype(BF16)
        fresh = bq_ref[...].astype(F32) - total[:, feat : feat + HD]
        bpad[...] = jnp.zeros_like(bpad)
        bpad[pl.ds(kv_cols, rank), :] = fresh.astype(BF16)

    def merge():
        loads[2]().wait()
        collect(3, 0)

        def rows_of(j):
            rows = pl.ds(pl.multiple_of(j * HD, HD), HD)
            product = lax.dot_general(
                aot[0, j], bo[...], (((0,), (0,)), ((), ())), preferred_element_type=F32
            )
            merged[rows, :] = (merged[rows, :].astype(F32) + product).astype(BF16)

        loop(0, n, rows_of)

    def attend(m):
        collect(1, m)
        query = scaled_q[...]
        for k in range(n_dp):
            query = query + jnp.dot(kvx[m, 2 * k + t], bpad[...], preferred_element_type=F32)
        query = query.astype(BF16)
        per = HD // kv_cols
        first = me // GROUP * 2 * per
        spot = lax.broadcasted_iota(jnp.int32, (HD, HD), 0)
        lane = lax.broadcasted_iota(jnp.int32, (HD, HD), 1)
        keys = jnp.zeros((tok, HD), F32)
        values = jnp.zeros((tok, HD), F32)
        for i in range(per):
            pick = jnp.where((spot < kv_cols) & (lane == spot + i * kv_cols), 1.0, 0.0).astype(BF16)
            keys = keys + jnp.dot(kvx[m, first + i], pick, preferred_element_type=F32)
            values = values + jnp.dot(kvx[m, first + per + i], pick, preferred_element_type=F32)
        scores = lax.dot_general(
            query, keys.astype(BF16), (((1,), (1,)), ((), ())), preferred_element_type=F32
        ) * HD ** (-0.5)
        here = lax.broadcasted_iota(jnp.int32, (tok, tok), 0)
        there = lax.broadcasted_iota(jnp.int32, (tok, tok), 1)
        visible = (there <= here) & (ends_ref[m] >= here)
        scores = jnp.where(visible, scores, -1e30)
        raised = jnp.exp(scores - jnp.max(scores, axis=-1, keepdims=True))
        portion = (raised / jnp.sum(raised, axis=-1, keepdims=True)).astype(BF16)
        mixed = jnp.dot(portion, values.astype(BF16), preferred_element_type=F32)
        mix[m, me] = mixed.astype(BF16)
        share(2, m)

    def leave(m):
        collect(2, m)
        heads = jnp.concatenate([mix[m, j] for j in range(n)], axis=1)
        total = jnp.dot(heads, merged[...], preferred_element_type=F32)
        out_ref[m] = (hidden[m].astype(F32) + total).astype(BF16)

        @pl.when(s < n_section - 1)
        def _():
            onward(m, after).start()
            if m == last:
                gain_landed()
                upper = out_ref[m, pl.ds(0, cut), :].astype(F32)
                help_out[d, pl.ds(0, cut), :] = (upper * gnext[:1]).astype(BF16)
                loop(1, n_dp, lambda k: help_copy(help_out, next_send, next_recv, k, 0).start())

                def relay(k):
                    help_landed(help_out, next_send, next_recv, k, 0)
                    help_on(help_out, next_on, k, 0, after).start()

                loop(1, n_dp, relay)

    @pl.when(s == 0)
    def _():
        for m in range(micro):
            entering(m).start()

    for k in (5, 6, 7, 4, 3, 1, 0, 2, 8, 9, 10):
        loads[k]().start()
    gown[...] = jnp.broadcast_to(gain_ref[...].astype(F32), gown.shape)
    barrier = pltpu.get_barrier_semaphore()

    def greet(k):
        i = lax.rem(me + k, n)
        to = {"dp": i // 2, "tensor": lax.rem(i, 2)}
        pl.semaphore_signal(barrier, inc=1, device_id=to, device_id_type=MESH)

    loop(1, n, greet)
    pl.semaphore_signal(barrier, inc=1, device_id={"groups": 1 - y}, device_id_type=MESH)

    @pl.when(s > 0)
    def _():
        pl.semaphore_signal(barrier, inc=1, device_id={"section": s - 1}, device_id_type=MESH)

    @pl.when(s < n_section - 1)
    def _():
        pl.semaphore_signal(barrier, inc=1, device_id={"section": s + 1}, device_id_type=MESH)

    sections = (s > 0).astype(jnp.int32) + (s < n_section - 1).astype(jnp.int32)
    pl.semaphore_wait(barrier, n + sections)

    @pl.when(s == 0)
    def _():
        for m in range(micro):
            enter_first(m)

    @pl.when(s > 0)
    def _():
        gain_copy().start()

    @pl.when(s == 1)
    def _():
        remote(blocks.at[last, me], help_in.at[d], hop_send, hop_recv, {"section": 0}).wait_recv()
        for part in range(2):
            loop(1, n_dp, lambda k: help_copy(help_in, in_send, in_recv, k, part).start())

    give_grads()
    join_weights()

    @pl.when(s == 1)
    def _():
        for part in range(2):

            def relay(k):
                help_landed(help_in, in_send, in_recv, k, part)
                help_on(help_in, in_on, k, part, 0).start()

            loop(1, n_dp, relay)

    @pl.when(s > 0)
    def _():
        enter_later(0)
        update()
        merge()

    for m in range(micro):
        project(m)
        if m == 0:

            @pl.when(s == 0)
            def _():
                update()

        if m + 1 < micro:

            @pl.when(s > 0)
            def _(m=m):
                enter_later(m + 1)

        attend(m)
        if m == 0:

            @pl.when(s == 0)
            def _():
                merge()

        leave(m)

    loop(1, n_dp, lambda k: grads(k).wait_send())
    sums(y).wait_send()
    sent(3, 0)
    for m in range(micro):
        for kind in range(3):
            sent(kind, m)
        sent(4, m, m < last)

    @pl.when(s == 0)
    def _():
        hop().wait_send()

    @pl.when(s == 1)
    def _():
        for part in range(2):
            loop(1, n_dp, lambda k: help_copy(help_in, in_send, in_recv, k, part).wait_send())
            loop(1, n_dp, lambda k: help_on(help_in, in_on, k, part, 0).wait_send())

    @pl.when(s > 0)
    def _():
        gain_copy().wait_send()
        loop(1, n_dp, lambda k: lower(k).wait_send())

    @pl.when(s < n_section - 1)
    def _():
        for m in range(micro):
            onward(m, after).wait_send()
        loop(1, n_dp, lambda k: help_copy(help_out, next_send, next_recv, k, 0).wait_send())
        loop(1, n_dp, lambda k: help_on(help_out, next_on, k, 0, after).wait_send())


def on_device(
    x_in,
    subtree_end,
    norm_gain,
    w_query,
    w_kv,
    w_out,
    a_query,
    b_query,
    a_out,
    b_out,
    grad_a_query,
    grad_b_query,
    grad_a_out,
    grad_b_out,
):
    n_dp, n_section = lax.axis_size("dp"), lax.axis_size("section")
    n = 2 * n_dp
    micro, tok, feat = x_in.shape
    width, kv_cols = w_kv.shape[1:]
    rank = a_query.shape[2]
    vmem = pl.BlockSpec(memory_space=pltpu.VMEM)
    hbm = pl.BlockSpec(memory_space=pltpu.HBM)
    dma = pltpu.SemaphoreType.DMA
    extra = feat + 2 * HD

    def exchange(count):
        return (dma((count, n_dp)), dma((count, n_dp)), dma((count, n)))

    return pl.pallas_call(
        functools.partial(chain, (n_dp, n_section, kv_cols)),
        out_shape=jax.ShapeDtypeStruct((micro, tok, feat), BF16),
        in_specs=[vmem] * 2 + [hbm] * 12,
        out_specs=vmem,
        scratch_shapes=[
            pltpu.VMEM((width, 2 * HD), BF16),
            pltpu.VMEM((HD, width), BF16),
            pltpu.VMEM((rank, width), BF16),
            pltpu.VMEM((rank, width), F32),
            pltpu.VMEM((rank, width), F32),
            pltpu.VMEM((rank, feat), BF16),
            pltpu.VMEM((rank, HD), BF16),
            pltpu.VMEM((rank, n * HD), BF16),
            pltpu.VMEM((rank, n * HD), F32),
            pltpu.VMEM((rank, n * HD), F32),
            pltpu.VMEM((n * HD, feat), BF16),
            pltpu.VMEM((micro, n, tok, feat), BF16),
            pltpu.VMEM((micro, n, 8, HD), F32),
            pltpu.VMEM((micro, tok, feat), BF16),
            pltpu.VMEM((micro, n, tok, HD), BF16),
            pltpu.VMEM((micro, n, tok, HD), BF16),
            pltpu.VMEM((1, n, rank, HD), BF16),
            pltpu.VMEM((n, rank, extra), BF16),
            pltpu.VMEM((n_dp, rank, extra), BF16),
            pltpu.VMEM((2, rank // 2, extra), BF16),
            pltpu.VMEM((n_dp, tok, feat), BF16),
            pltpu.VMEM((n_dp, tok, feat), BF16),
            pltpu.VMEM((8, feat), F32),
            pltpu.VMEM((8, feat), F32),
            pltpu.VMEM((rank, feat), BF16),
            pltpu.VMEM((HD, HD), BF16),
            pltpu.VMEM((tok, 2 * HD), F32),
            pltpu.VMEM((tok, HD), F32),
            dma((11,)),
            exchange(micro),
            exchange(micro),
            exchange(micro),
            exchange(micro),
            exchange(1),
            dma((n_dp,)),
            dma((n_dp,)),
            dma,
            dma,
            dma((2, n_dp)),
            dma((2, n_dp)),
            dma((2, n_dp)),
            dma((2, n_dp)),
            dma((2, n_dp)),
            dma((2, n_dp)),
            dma((micro,)),
            dma((micro,)),
            dma((2,)),
            dma((2, n)),
            dma((n_dp,)),
            dma((3,)),
            dma((micro,)),
        ],
        compiler_params=pltpu.CompilerParams(
            collective_id=0, has_side_effects=True, vmem_limit_bytes=63 * 2**20
        ),
    )(
        subtree_end[:, None, :],
        norm_gain,
        x_in,
        b_out[0],
        b_query[0],
        a_out[0].T,
        grad_b_query[0, 0],
        grad_a_out[0, 0].T,
        grad_b_out[0, 0],
        a_query[0].T,
        grad_a_query[0, 0].T,
        w_query[0],
        w_kv[0].T,
        w_out[0],
    )[None]


def solution(mesh):
    placed = (
        P("groups", None, ("dp", "tensor")),
        P("groups", None),
        P("section", ("dp", "tensor")),
        P("section", None, ("dp", "tensor")),
        P("section", None, ("dp", "tensor")),
        P("section", None, ("dp", "tensor")),
        P("section", None, None),
        P("section", None, ("dp", "tensor")),
        P("section", None, None),
        P("section", None, ("dp", "tensor")),
        P("section", "dp", None, None),
        P("section", "dp", None, None),
        P("section", "dp", None, None),
        P("section", "dp", None, None),
    )
    return jax.shard_map(
        on_device,
        mesh=mesh,
        in_specs=placed,
        out_specs=P("section", "groups", None, ("dp", "tensor")),
        check_vma=False,
    )
```
